32 devices in a mesh: expert: 8 (over y, x, core), tensor: 4 (over z).
Axes of the slice: x: 2, y: 2, z: 4, core: 2. Of those that a mesh axis runs over, the one named last changes fastest.
Arguments:
- tokens: bfloat16 [1024, 7168], P(('expert', 'tensor')), may hold values from -54 to 54
- dense_in: bfloat16 [2, 2432, 7168], P(None, 'tensor'), may hold values from -1 to 1
- dense_out: bfloat16 [2432, 7168], P('tensor'), may hold values from -1 to 1
- expert_in: bfloat16 [8, 2, 2432, 7168], P('expert', None, 'tensor'), may hold values from -1 to 1
- expert_out: bfloat16 [8, 2432, 7168], P('expert', 'tensor'), may hold values from -1 to 1
- norm_gains: float32 [3, 7168], replicated, may hold values from 0 to 2
- expert_ids: int32 [1024, 2], P('expert'), may hold values from 0 to 7, as said below
- gate_probs: float32 [1024, 2], P('expert'), may hold values from 0 to 1
- cotangent: bfloat16 [1024, 7168], P(('expert', 'tensor')), may hold values from -6 to 6
Outputs:
- layer_output: bfloat16 [1024, 7168], P(('expert', 'tensor'))
- input_grad: bfloat16 [1024, 7168], P(('expert', 'tensor'))
The draws below stay inside these ranges and needn't reach their ends.
Inputs may be any that keep to these rules, and one draw needn't show every extreme that they name: `expert_ids`: the ids of one row differ; in each aligned block of 128 rows (the tokens of one index of expert) no id stands in more than 48 rows, and some id in exactly 48; every id stands in every block.
All inputs are finite; a program needn't handle non-finite values.
Results may differ from the reference program's by a relative error of at most 0.028.
Values may be sent and summed in bfloat16 or wider, within the bound.
A program may use at most 128 MiB of HBM per device.

```python
import math
import jax
import jax.numpy as jnp
from jax import lax

D = 7168
FF_WIN = 2432
EX_WIN = 2432
TOP = 2
TOK_GRP = 128
EXPERTS = 8
CAP = 48
TOKENS = 1024
N_EXPERT = 8
N_TENSOR = 4


epsilon = 1e-05


def tokens_values(key):
    key_row, key_col, key_base, key_mean = jax.random.split(jax.random.fold_in(key, 101), 4)
    lowest = math.log(0.3)
    highest = math.log(3.0)
    row_scale = jnp.exp(jax.random.uniform(key_row, (TOKENS, 1), jnp.float32, lowest, highest))
    col_scale = jnp.exp(jax.random.uniform(key_col, (1, D), jnp.float32, lowest, highest))
    base_draw = jnp.clip(jax.random.normal(key_base, (TOKENS, D), jnp.float32), -6.0, 6.0)
    return (base_draw * row_scale * col_scale).astype(jnp.bfloat16)


def weight_values(key, shape, fan_in):
    return (jnp.clip(jax.random.normal(key, shape, jnp.float32), -6.0, 6.0) * fan_in ** (-0.5)).astype(jnp.bfloat16)


def dense_in_values(key):
    return weight_values(jax.random.fold_in(key, 201), (2, FF_WIN, D), D)


def dense_out_values(key):
    return weight_values(jax.random.fold_in(key, 202), (FF_WIN, D), FF_WIN)


def expert_in_values(key, expert_index):
    return weight_values(jax.random.fold_in(jax.random.fold_in(key, 203), expert_index), (2, EX_WIN, D), D)


def expert_out_values(key, expert_index):
    return weight_values(jax.random.fold_in(jax.random.fold_in(key, 204), expert_index), (EX_WIN, D), EX_WIN)


def gain_values(key):
    spread = jnp.clip(jax.random.normal(jax.random.fold_in(key, 205), (3, D), jnp.float32), -5.0, 5.0)
    return 1.0 + 0.1 * spread


def gate_values(key):
    return jax.random.uniform(jax.random.fold_in(key, 206), (TOKENS, TOP), jnp.float32, 0.05, 1.0)


def route_table(key):
    route_key = jax.random.fold_in(key, 207)
    heavy = EXPERTS // 4
    others = EXPERTS - heavy
    rest = TOP * TOK_GRP - heavy * CAP
    rank = jnp.arange(EXPERTS, dtype=jnp.int32)
    lighter = rest // others + (rank - heavy < rest % others).astype(jnp.int32)
    loads = jnp.where(rank < heavy, CAP, lighter).astype(jnp.int32)
    bounds = jnp.cumsum(loads).astype(jnp.int32)
    spots = jnp.arange(TOP * TOK_GRP, dtype=jnp.int32)
    label_rank = jnp.sum((spots[:, None] >= bounds[None, :]).astype(jnp.int32), axis=1).astype(jnp.int32)
    blocks = TOKENS // TOK_GRP

    def one_block(index):
        block_key = jax.random.fold_in(route_key, index)
        key_perm, key_rows, key_flip = jax.random.split(block_key, 3)
        relabel = jax.random.permutation(key_perm, EXPERTS).astype(jnp.int32)
        labels = jnp.take(relabel, label_rank).reshape(TOP, TOK_GRP).T
        order = jax.random.permutation(key_rows, TOK_GRP).astype(jnp.int32)
        rows = jnp.take(labels, order, axis=0)
        flip = jax.random.randint(key_flip, (TOK_GRP, 1), 0, 2)
        return jnp.where(flip == 1, rows[:, ::-1], rows).astype(jnp.int32)
    table = jax.vmap(one_block)(jnp.arange(blocks, dtype=jnp.int32))
    return table.reshape(TOKENS, TOP).astype(jnp.int32)


def rms_scale_drawn(values):
    return lax.rsqrt(jnp.mean(values * values, axis=-1, keepdims=True) + epsilon)


def slot_table_drawn(group_ids, experts, capacity):
    routes = group_ids.reshape(-1)
    route_total = routes.shape[0]
    onehot = (routes[:, None] == jnp.arange(experts, dtype=jnp.int32)[None, :]).astype(jnp.int32)
    earlier = jnp.cumsum(onehot, axis=0) - onehot
    slot_index = jnp.sum(earlier * onehot, axis=1).astype(jnp.int32)
    position = (routes * capacity + slot_index).astype(jnp.int32)
    inverse = jnp.full((experts * capacity,), route_total, jnp.int32)
    inverse = inverse.at[position].set(jnp.arange(route_total, dtype=jnp.int32))
    return (position, inverse)


def take_rows_drawn(values, index_rows):
    return jnp.take(values, index_rows.astype(jnp.int32), axis=0)


def branch_outputs(key):
    groups = TOKENS // TOK_GRP
    source = tokens_values(key).astype(jnp.float32)
    gains = gain_values(key)
    normed = (source * rms_scale_drawn(source) * gains[0]).astype(jnp.bfloat16).astype(jnp.float32)
    weights_in = dense_in_values(key).astype(jnp.float32)
    preact = jnp.einsum('td,khd->tkh', normed, weights_in)
    hidden = (jax.nn.silu(preact[:, 0]) * preact[:, 1]).astype(jnp.bfloat16).astype(jnp.float32)
    dense_raw = jnp.dot(hidden, dense_out_values(key).astype(jnp.float32))
    ids = route_table(key)
    probs = gate_values(key)

    def table_one(group_ids):
        return slot_table_drawn(group_ids, EXPERTS, CAP)
    position, inverse = jax.vmap(table_one)(ids.reshape(groups, TOK_GRP, TOP))
    routed = jnp.repeat(normed.reshape(groups, TOK_GRP, D), TOP, axis=1)
    routed = jnp.concatenate([routed, jnp.zeros((groups, 1, D), jnp.float32)], axis=1)
    picked = jax.vmap(take_rows_drawn)(routed, inverse)
    picked = picked.reshape(groups, EXPERTS, CAP, D).transpose(1, 0, 2, 3).reshape(EXPERTS, groups * CAP, D)

    def per_expert(operands):
        expert_index, operand_rows = operands
        expert_weights = expert_in_values(key, expert_index).astype(jnp.float32)
        expert_pre = jnp.einsum('rd,khd->rkh', operand_rows, expert_weights)
        expert_hidden = (jax.nn.silu(expert_pre[:, 0]) * expert_pre[:, 1]).astype(jnp.bfloat16).astype(jnp.float32)
        return jnp.dot(expert_hidden, expert_out_values(key, expert_index).astype(jnp.float32))
    outputs = lax.map(per_expert, (jnp.arange(EXPERTS, dtype=jnp.int32), picked))
    regrouped = outputs.reshape(EXPERTS, groups, CAP, D).transpose(1, 0, 2, 3).reshape(groups, EXPERTS * CAP, D)
    back_rows = jax.vmap(take_rows_drawn)(regrouped, position).reshape(groups, TOK_GRP, TOP, D)
    mixture_raw = jnp.sum(back_rows * probs.reshape(groups, TOK_GRP, TOP, 1), axis=2).reshape(TOKENS, D)
    return (dense_raw, mixture_raw)


def draw_tokens(key, part):
    return tokens_values(key)


def draw_dense_in(key, part):
    return dense_in_values(key)


def draw_dense_out(key, part):
    return dense_out_values(key)


def draw_expert_in(key, part):
    return lax.map(lambda expert_index: expert_in_values(key, expert_index), jnp.arange(EXPERTS, dtype=jnp.int32))


def draw_expert_out(key, part):
    return lax.map(lambda expert_index: expert_out_values(key, expert_index), jnp.arange(EXPERTS, dtype=jnp.int32))


def draw_norm_gains(key, part):
    return gain_values(key)


def draw_expert_ids(key, part):
    return route_table(key)


def draw_gate_probs(key, part):
    return gate_values(key)


def draw_cotangent(key, part):
    dense_raw, mixture_raw = branch_outputs(key)
    dense_unit = dense_raw * rms_scale_drawn(dense_raw)
    mixture_unit = mixture_raw * rms_scale_drawn(mixture_raw)
    noise_key = jax.random.fold_in(key, 208)
    noise = jnp.clip(jax.random.normal(noise_key, (TOKENS, D), jnp.float32), -6.0, 6.0)
    combined = 0.5 * noise + dense_unit + mixture_unit
    return jnp.clip(combined, -6.0, 6.0).astype(jnp.bfloat16)


def setup_inputs(seed: int = 0) -> dict:
    streams_of = jax.random.split(jax.random.key(seed), 10)
    tokens = draw_tokens(jax.random.fold_in(streams_of[9], 71), 0)
    dense_in = draw_dense_in(jax.random.fold_in(streams_of[9], 71), 0)
    dense_out = draw_dense_out(jax.random.fold_in(streams_of[9], 71), 0)
    expert_in = draw_expert_in(jax.random.fold_in(streams_of[9], 71), 0)
    expert_out = draw_expert_out(jax.random.fold_in(streams_of[9], 71), 0)
    norm_gains = draw_norm_gains(jax.random.fold_in(streams_of[9], 71), 0)
    expert_ids = draw_expert_ids(jax.random.fold_in(streams_of[9], 71), 0)
    gate_probs = draw_gate_probs(jax.random.fold_in(streams_of[9], 71), 0)
    cotangent = draw_cotangent(jax.random.fold_in(streams_of[9], 71), 0)
    return {"tokens": tokens, "dense_in": dense_in, "dense_out": dense_out, "expert_in": expert_in, "expert_out": expert_out, "norm_gains": norm_gains, "expert_ids": expert_ids, "gate_probs": gate_probs, "cotangent": cotangent}


epsilon = 1e-05

def rms_scale(values):
    return lax.rsqrt(lax.optimization_barrier(jnp.mean(values * values, axis=-1, keepdims=True)) + epsilon)

def norm_grad(values, gain_row, upstream):
    factor = rms_scale(values)
    weighted = gain_row * upstream
    inner_mean = lax.optimization_barrier(jnp.mean(weighted * values, axis=-1, keepdims=True))
    return factor * weighted - values * factor * factor * factor * inner_mean

def silu_grad(preact):
    sigmoid_value = jax.nn.sigmoid(preact)
    return sigmoid_value * (1.0 + preact * (1.0 - sigmoid_value))

def slot_table(group_ids, experts, capacity):
    routes = group_ids.reshape(-1)
    route_total = routes.shape[0]
    onehot = (routes[:, None] == jnp.arange(experts, dtype=jnp.int32)[None, :]).astype(jnp.int32)
    earlier = jnp.cumsum(onehot, axis=0) - onehot
    slot_index = lax.optimization_barrier(jnp.sum(earlier * onehot, axis=1)).astype(jnp.int32)
    position = (routes * capacity + slot_index).astype(jnp.int32)
    inverse = jnp.full((experts * capacity,), route_total, jnp.int32)
    inverse = inverse.at[position].set(jnp.arange(route_total, dtype=jnp.int32))
    return (position, inverse)

def take_rows(values, index_rows):
    return jnp.take(values, index_rows.astype(jnp.int32), axis=0)

def reference(tokens, dense_in, dense_out, expert_in, expert_out, norm_gains, expert_ids, gate_probs, cotangent):
    groups = N_EXPERT
    block_width = EX_WIN // N_TENSOR
    route_count = TOK_GRP * TOP
    source = tokens.astype(jnp.float32)
    normed = (source * rms_scale(source) * norm_gains[0]).astype(jnp.bfloat16)
    preact_dense = jnp.einsum('td,khd->tkh', normed.astype(jnp.float32), dense_in.astype(jnp.float32))
    hidden_dense = (jax.nn.silu(preact_dense[:, 0]) * preact_dense[:, 1]).astype(jnp.bfloat16)
    dense_raw = jnp.dot(hidden_dense, dense_out, preferred_element_type=jnp.float32)

    def table_one(group_ids):
        return slot_table(group_ids, EXPERTS, CAP)
    position, inverse = jax.vmap(table_one)(expert_ids.reshape(groups, TOK_GRP, TOP))
    gates_grouped = gate_probs.reshape(groups, TOK_GRP, TOP, 1)

    def with_empty(values):
        return jnp.concatenate([values, jnp.zeros((groups, 1, D), values.dtype)], axis=1)

    def to_experts(values):
        picked = jax.vmap(take_rows)(values, inverse)
        picked = picked.reshape(groups, EXPERTS, CAP, D).transpose(1, 0, 2, 3)
        return picked.reshape(EXPERTS, groups * CAP, D)

    def from_experts(values):
        regrouped = values.reshape(EXPERTS, groups, CAP, D).transpose(1, 0, 2, 3)
        regrouped = regrouped.reshape(groups, EXPERTS * CAP, D)
        return jax.vmap(take_rows)(regrouped, position).reshape(groups, TOK_GRP, TOP, D)

    def block_sum(hidden, weight_rows):
        blocked = hidden.astype(jnp.float32).reshape(hidden.shape[0], N_TENSOR, block_width)
        partial_value = jnp.einsum('rsh,shd->rsd', blocked, weight_rows.astype(jnp.float32).reshape(N_TENSOR, block_width, D))
        return partial_value

    def finish_blocks(partial_value):
        rounded = lax.optimization_barrier(partial_value.astype(jnp.bfloat16))
        return lax.optimization_barrier(jnp.sum(rounded.astype(jnp.float32), axis=1))
    routes_forward = jnp.repeat(normed.reshape(groups, TOK_GRP, D), TOP, axis=1)
    buffers = to_experts(with_empty(routes_forward))

    def expert_forward(operands):
        operand_rows, weight_in, weight_out = operands
        preact = jnp.einsum('rd,khd->rkh', operand_rows.astype(jnp.float32), weight_in.astype(jnp.float32))
        hidden = (jax.nn.silu(preact[:, 0]) * preact[:, 1]).astype(jnp.bfloat16)
        return (finish_blocks(block_sum(hidden, weight_out)), preact)
    expert_output, preact_expert = lax.map(expert_forward, (buffers, expert_in, expert_out))
    routed_output = from_experts(expert_output)
    mixture_raw = lax.optimization_barrier(jnp.sum(routed_output * gates_grouped, axis=2)).reshape(TOKENS, D)
    layer_output = (source + dense_raw * rms_scale(dense_raw) * norm_gains[1] + mixture_raw * rms_scale(mixture_raw) * norm_gains[2]).astype(jnp.bfloat16)
    upstream = cotangent.astype(jnp.float32)
    dense_grad = norm_grad(dense_raw, norm_gains[1], upstream).astype(jnp.bfloat16)
    mixture_grad = norm_grad(mixture_raw, norm_gains[2], upstream).astype(jnp.bfloat16)
    back_dense = jnp.dot(dense_grad, dense_out.T, preferred_element_type=jnp.float32)
    gate_dense = (back_dense * preact_dense[:, 1] * silu_grad(preact_dense[:, 0])).astype(jnp.bfloat16)
    up_dense = (back_dense * jax.nn.silu(preact_dense[:, 0])).astype(jnp.bfloat16)
    dense_input = jnp.dot(gate_dense, dense_in[0], preferred_element_type=jnp.float32) + jnp.dot(up_dense, dense_in[1], preferred_element_type=jnp.float32)
    routed_grad = (gates_grouped * mixture_grad.reshape(groups, TOK_GRP, 1, D).astype(jnp.float32)).astype(jnp.bfloat16)
    grad_buffers = to_experts(with_empty(routed_grad.reshape(groups, route_count, D)))

    def expert_backward(operands):
        operand_rows, preact, weight_in, weight_out = operands
        back_rows = jnp.dot(operand_rows, weight_out.T, preferred_element_type=jnp.float32)
        gate_part = (back_rows * preact[:, 1] * silu_grad(preact[:, 0])).astype(jnp.bfloat16)
        up_part = (back_rows * jax.nn.silu(preact[:, 0])).astype(jnp.bfloat16)
        partial_value = block_sum(gate_part, weight_in[0]) + block_sum(up_part, weight_in[1])
        return finish_blocks(partial_value)
    expert_input = lax.map(expert_backward, (grad_buffers, preact_expert, expert_in, expert_out))
    mixture_input = lax.optimization_barrier(jnp.sum(from_experts(expert_input), axis=2)).reshape(TOKENS, D)
    input_grad = norm_grad(source, norm_gains[0], dense_input + mixture_input).astype(jnp.bfloat16)
    return (layer_output, input_grad)
```

```python
import jax
import jax.numpy as jnp
from jax import lax
from jax.sharding import PartitionSpec as P

epsilon = 1e-05


def rms_scale(values):
    return lax.rsqrt(jnp.mean(values * values, axis=-1, keepdims=True) + epsilon)


def norm_grad(values, gain_row, upstream):
    factor = rms_scale(values)
    weighted = gain_row * upstream
    inner_mean = jnp.mean(weighted * values, axis=-1, keepdims=True)
    return factor * weighted - values * factor * factor * factor * inner_mean


def silu_grad(preact):
    sigmoid_value = jax.nn.sigmoid(preact)
    return sigmoid_value * (1.0 + preact * (1.0 - sigmoid_value))


def route_matrices(group_ids, gates, experts, capacity):
    routes = group_ids.reshape(-1)
    order = jnp.arange(routes.shape[0], dtype=jnp.int32)
    earlier = (routes[:, None] == routes[None, :]) & (order[None, :] < order[:, None])
    slot_index = jnp.sum(earlier.astype(jnp.int32), axis=1)
    position = (routes * capacity + slot_index).reshape(group_ids.shape)
    slots = jnp.arange(experts * capacity, dtype=jnp.int32)
    held = (position[:, :, None] == slots[None, None, :]).astype(jnp.float32)
    pick = jnp.sum(held, axis=1).astype(jnp.bfloat16)
    mix = jnp.sum(held * gates[:, :, None], axis=1)
    return pick, mix.astype(jnp.bfloat16), jnp.sum(mix, axis=0)


def per_device(
    tokens,
    dense_in,
    dense_out,
    expert_in,
    expert_out,
    norm_gains,
    expert_ids,
    gate_probs,
    cotangent,
):
    experts = lax.axis_size("expert") * expert_in.shape[0]
    group_rows = expert_ids.shape[0]
    top_count = expert_ids.shape[1]
    capacity = 3 * group_rows * top_count // (2 * experts)
    model_width = tokens.shape[1]
    weight_in = expert_in[0]
    weight_out = expert_out[0]
    source = tokens.astype(jnp.float32)
    normed_local = (source * rms_scale(source) * norm_gains[0]).astype(jnp.bfloat16)
    normed = lax.all_gather(normed_local, "tensor", axis=0, tiled=True)
    preact_dense = jnp.einsum("gd,khd->gkh", normed, dense_in, preferred_element_type=jnp.float32)
    hidden_dense = (jax.nn.silu(preact_dense[:, 0]) * preact_dense[:, 1]).astype(jnp.bfloat16)
    dense_part = jnp.dot(hidden_dense, dense_out, preferred_element_type=jnp.float32)
    pick, mix, slot_gates = route_matrices(expert_ids, gate_probs, experts, capacity)
    buffer = jnp.einsum("gs,gd->sd", pick, normed, preferred_element_type=jnp.float32)
    buffer = buffer.astype(jnp.bfloat16).reshape(experts, capacity, model_width)
    preact = jnp.einsum(
        "scd,khd->sckh",
        lax.all_to_all(buffer, "expert", split_axis=0, concat_axis=0, tiled=True),
        weight_in,
        preferred_element_type=jnp.float32,
    )
    hidden = (jax.nn.silu(preact[:, :, 0]) * preact[:, :, 1]).astype(jnp.bfloat16)
    partial_value = jnp.einsum(
        "sch,hd->scd", hidden, weight_out, preferred_element_type=jnp.float32
    )
    partial_value, preact_expert = (partial_value.astype(jnp.bfloat16), preact)
    returned = lax.all_to_all(partial_value, "expert", split_axis=0, concat_axis=0, tiled=True)
    returned = returned.reshape(experts * capacity, model_width)
    mixture_part = jnp.dot(mix, returned, preferred_element_type=jnp.float32)
    dense_raw, mixture_raw = (
        lax.psum_scatter(
            dense_part.astype(jnp.bfloat16), "tensor", scatter_dimension=0, tiled=True
        ).astype(jnp.float32),
        lax.psum_scatter(
            mixture_part.astype(jnp.bfloat16), "tensor", scatter_dimension=0, tiled=True
        ).astype(jnp.float32),
    )
    layer_output = (
        source
        + dense_raw * rms_scale(dense_raw) * norm_gains[1]
        + mixture_raw * rms_scale(mixture_raw) * norm_gains[2]
    ).astype(jnp.bfloat16)
    upstream = cotangent.astype(jnp.float32)
    dense_grad = norm_grad(dense_raw, norm_gains[1], upstream).astype(jnp.bfloat16)
    mixture_grad = norm_grad(mixture_raw, norm_gains[2], upstream).astype(jnp.bfloat16)
    dense_rows, mixture_rows = (
        lax.all_gather(dense_grad, "tensor", axis=0, tiled=True),
        lax.all_gather(mixture_grad, "tensor", axis=0, tiled=True),
    )
    back_dense = jnp.einsum("gd,hd->gh", dense_rows, dense_out, preferred_element_type=jnp.float32)
    gate_dense = (back_dense * preact_dense[:, 1] * silu_grad(preact_dense[:, 0])).astype(
        jnp.bfloat16
    )
    up_dense = (back_dense * jax.nn.silu(preact_dense[:, 0])).astype(jnp.bfloat16)
    dense_input = jnp.dot(gate_dense, dense_in[0], preferred_element_type=jnp.float32) + jnp.dot(
        up_dense, dense_in[1], preferred_element_type=jnp.float32
    )
    grad_buffer = jnp.einsum("gs,gd->sd", pick, mixture_rows, preferred_element_type=jnp.float32)
    grad_buffer = (grad_buffer * slot_gates[:, None]).astype(jnp.bfloat16)
    grad_buffer = grad_buffer.reshape(experts, capacity, model_width)
    back_expert = jnp.einsum(
        "scd,hd->sch",
        lax.all_to_all(grad_buffer, "expert", split_axis=0, concat_axis=0, tiled=True),
        weight_out,
        preferred_element_type=jnp.float32,
    )
    gate_expert = (back_expert * preact_expert[:, :, 1] * silu_grad(preact_expert[:, :, 0])).astype(
        jnp.bfloat16
    )
    up_expert = (back_expert * jax.nn.silu(preact_expert[:, :, 0])).astype(jnp.bfloat16)
    input_part = (
        jnp.einsum("sch,hd->scd", gate_expert, weight_in[0], preferred_element_type=jnp.float32)
        + jnp.einsum("sch,hd->scd", up_expert, weight_in[1], preferred_element_type=jnp.float32)
    ).astype(jnp.bfloat16)
    returned_grad = lax.all_to_all(input_part, "expert", split_axis=0, concat_axis=0, tiled=True)
    returned_grad = returned_grad.reshape(experts * capacity, model_width)
    mixture_input = jnp.dot(pick, returned_grad, preferred_element_type=jnp.float32)
    input_total = lax.psum_scatter(
        (dense_input + mixture_input).astype(jnp.bfloat16),
        "tensor",
        scatter_dimension=0,
        tiled=True,
    ).astype(jnp.float32)
    input_grad = norm_grad(source, norm_gains[0], input_total).astype(jnp.bfloat16)
    return (layer_output, input_grad)


def solution(mesh):
    placed = (
        P(("expert", "tensor"), None),
        P(None, "tensor", None),
        P("tensor", None),
        P("expert", None, "tensor", None),
        P("expert", "tensor", None),
        P(),
        P("expert", None),
        P("expert", None),
        P(("expert", "tensor"), None),
    )
    return jax.shard_map(
        per_device,
        mesh=mesh,
        in_specs=placed,
        out_specs=(P(("expert", "tensor"), None), P(("expert", "tensor"), None)),
        check_vma=False,
    )
```

```python
import functools

import jax
import jax.numpy as jnp
from jax import lax
from jax.experimental import pallas as pl
from jax.experimental.pallas import tpu as pltpu
from jax.sharding import PartitionSpec as P

epsilon = 1e-05


def rms_scale(values):
    return lax.rsqrt(jnp.mean(values * values, axis=-1, keepdims=True) + epsilon)


def norm_grad(values, gain_row, upstream):
    factor = rms_scale(values)
    weighted = gain_row * upstream
    inner_mean = jnp.mean(weighted * values, axis=-1, keepdims=True)
    return factor * weighted - values * factor * factor * factor * inner_mean


def silu_grad(preact):
    sigmoid_value = jax.nn.sigmoid(preact)
    return sigmoid_value * (1.0 + preact * (1.0 - sigmoid_value))


def route_matrices(group_ids, gates, experts, capacity):
    routes = group_ids.reshape(-1)
    order = jnp.arange(routes.shape[0], dtype=jnp.int32)
    earlier = (routes[:, None] == routes[None, :]) & (order[None, :] < order[:, None])
    slot_index = jnp.sum(earlier.astype(jnp.int32), axis=1)
    position = (routes * capacity + slot_index).reshape(group_ids.shape)
    slots = jnp.arange(experts * capacity, dtype=jnp.int32)
    held = (position[:, :, None] == slots[None, None, :]).astype(jnp.float32)
    pick = jnp.sum(held, axis=1).astype(jnp.bfloat16)
    mix = jnp.sum(held * gates[:, :, None], axis=1)
    return pick, mix.astype(jnp.bfloat16), jnp.sum(mix, axis=0)


def spread_kernel(experts, ranks, chunks, separate, *refs):
    if separate:
        rows, pick, gates, extra, received, whole, *scratch = refs
    else:
        rows, pick, gates, received, whole, *scratch = refs
        extra = None
    staged, outgoing, z_send, z_recv, e_send, e_recv, w_send, w_recv, own_sem, stage_sem = scratch
    me, rank = lax.axis_index("expert"), lax.axis_index("tensor")
    mesh_id = pl.DeviceIdType.MESH
    width = rows.shape[1] // chunks
    group_rows = ranks * rows.shape[0]

    barrier = pltpu.get_barrier_semaphore()
    for k in range(1, ranks):
        pl.semaphore_signal(
            barrier, inc=1, device_id={"tensor": lax.rem(rank + k, ranks)}, device_id_type=mesh_id
        )
    for k in range(1, experts):
        pl.semaphore_signal(
            barrier, inc=1, device_id={"expert": lax.rem(me + k, experts)}, device_id_type=mesh_id
        )
    pl.semaphore_wait(barrier, ranks + experts - 2)

    def gather_copy(c, k, slot):
        cols = pl.ds(c * width, width)
        return pltpu.make_async_remote_copy(
            src_ref=rows.at[:, cols],
            dst_ref=staged.at[slot, :, cols],
            send_sem=z_send.at[c, k],
            recv_sem=z_recv.at[c, k],
            device_id={"tensor": lax.rem(rank + k, ranks)},
            device_id_type=mesh_id,
        )

    def expert_copy(c, k, slot):
        cols = pl.ds(c * width, width)
        target = lax.rem(me + k, experts)
        return pltpu.make_async_remote_copy(
            src_ref=outgoing.at[target, :, cols],
            dst_ref=received.at[slot, :, cols],
            send_sem=e_send.at[c, k],
            recv_sem=e_recv.at[c, k],
            device_id={"expert": target},
            device_id_type=mesh_id,
        )

    def extra_copy(k, slot):
        return pltpu.make_async_remote_copy(
            src_ref=extra,
            dst_ref=whole.at[slot],
            send_sem=w_send.at[k],
            recv_sem=w_recv.at[k],
            device_id={"tensor": lax.rem(rank + k, ranks)},
            device_id_type=mesh_id,
        )

    for c in range(chunks):
        for k in range(1, ranks):
            gather_copy(c, k, rank).start()
    staged[rank] = rows[...]
    for c in range(chunks):
        cols = slice(c * width, (c + 1) * width)
        for k in range(1, ranks):
            gather_copy(c, k, lax.rem(rank + ranks - k, ranks)).wait_recv()
        if c == chunks - 1:
            if separate:
                for k in range(1, ranks):
                    extra_copy(k, rank).start()
                stage_copy = pltpu.make_async_copy(extra, whole.at[rank], stage_sem)
            else:
                stage_copy = pltpu.make_async_copy(staged, whole, stage_sem)
            stage_copy.start()
        block = staged[:, :, cols].reshape(group_rows, width)

        def fill(target):
            value = jnp.dot(pick[target], block, preferred_element_type=jnp.float32)
            if separate:
                value = value * gates[target]
            outgoing[target, :, cols] = value.astype(outgoing.dtype)

        def step(k, carry):
            fill(lax.rem(me + k, experts))
            expert_copy(c, k, me).start()
            return carry

        lax.fori_loop(1, experts, step, 0)
        fill(me)
    own_copy = pltpu.make_async_copy(outgoing.at[me], received.at[me], own_sem)
    own_copy.start()
    for c in range(chunks):
        for k in range(1, ranks):
            gather_copy(c, k, rank).wait_send()

        def finish(k, carry):
            copy = expert_copy(c, k, lax.rem(me + experts - k, experts))
            copy.wait_send()
            copy.wait_recv()
            return carry

        lax.fori_loop(1, experts, finish, 0)
    if separate:
        for k in range(1, ranks):
            copy = extra_copy(k, lax.rem(rank + ranks - k, ranks))
            copy.wait_send()
            copy.wait_recv()
    stage_copy.wait()
    own_copy.wait()


def spread(rows, pick, gates, extra, experts, collective_id):
    ranks = lax.axis_size("tensor")
    count, model_width = rows.shape
    capacity = pick.shape[1] // experts
    chunks = 4 if model_width % 512 == 0 else 1
    separate = extra is not None
    dma = pltpu.SemaphoreType.DMA
    operands = [
        rows,
        pick.T.reshape(experts, capacity, pick.shape[0]),
        gates.reshape(experts, capacity, 1),
    ]
    if separate:
        operands.append(extra)
    received, whole = pl.pallas_call(
        functools.partial(spread_kernel, experts, ranks, chunks, separate),
        out_shape=(
            jax.ShapeDtypeStruct((experts, capacity, model_width), rows.dtype),
            jax.ShapeDtypeStruct((ranks, count, model_width), rows.dtype),
        ),
        in_specs=[pl.BlockSpec(memory_space=pltpu.VMEM)] * len(operands),
        out_specs=(pl.BlockSpec(memory_space=pl.ANY), pl.BlockSpec(memory_space=pl.ANY)),
        scratch_shapes=[
            pltpu.VMEM((ranks, count, model_width), rows.dtype),
            pltpu.VMEM((experts, capacity, model_width), rows.dtype),
            dma((chunks, ranks)),
            dma((chunks, ranks)),
            dma((chunks, experts)),
            dma((chunks, experts)),
            dma((ranks,)),
            dma((ranks,)),
            dma(()),
            dma(()),
        ],
        compiler_params=pltpu.CompilerParams(
            collective_id=collective_id, has_side_effects=True, vmem_limit_bytes=40 * 1024 * 1024
        ),
    )(*operands)
    return received, whole.reshape(ranks * count, model_width)


def per_device(
    tokens,
    dense_in,
    dense_out,
    expert_in,
    expert_out,
    norm_gains,
    expert_ids,
    gate_probs,
    cotangent,
):
    experts = lax.axis_size("expert") * expert_in.shape[0]
    group_rows = expert_ids.shape[0]
    top_count = expert_ids.shape[1]
    capacity = 3 * group_rows * top_count // (2 * experts)
    model_width = tokens.shape[1]
    weight_in = expert_in[0]
    weight_out = expert_out[0]
    source = tokens.astype(jnp.float32)
    normed_local = (source * rms_scale(source) * norm_gains[0]).astype(jnp.bfloat16)
    pick, mix, slot_gates = route_matrices(expert_ids, gate_probs, experts, capacity)
    arrived, normed = spread(normed_local, pick, slot_gates, None, experts, 0)
    preact_dense = jnp.einsum("gd,khd->gkh", normed, dense_in, preferred_element_type=jnp.float32)
    hidden_dense = (jax.nn.silu(preact_dense[:, 0]) * preact_dense[:, 1]).astype(jnp.bfloat16)
    dense_part = jnp.dot(hidden_dense, dense_out, preferred_element_type=jnp.float32)
    preact = jnp.einsum(
        "scd,khd->sckh",
        arrived,
        weight_in,
        preferred_element_type=jnp.float32,
    )
    hidden = (jax.nn.silu(preact[:, :, 0]) * preact[:, :, 1]).astype(jnp.bfloat16)
    partial_value = jnp.einsum(
        "sch,hd->scd", hidden, weight_out, preferred_element_type=jnp.float32
    )
    partial_value, preact_expert = (partial_value.astype(jnp.bfloat16), preact)
    returned = lax.all_to_all(partial_value, "expert", split_axis=0, concat_axis=0, tiled=True)
    returned = returned.reshape(experts * capacity, model_width)
    mixture_part = jnp.dot(mix, returned, preferred_element_type=jnp.float32)
    dense_raw, mixture_raw = (
        lax.psum_scatter(
            dense_part.astype(jnp.bfloat16), "tensor", scatter_dimension=0, tiled=True
        ).astype(jnp.float32),
        lax.psum_scatter(
            mixture_part.astype(jnp.bfloat16), "tensor", scatter_dimension=0, tiled=True
        ).astype(jnp.float32),
    )
    layer_output = (
        source
        + dense_raw * rms_scale(dense_raw) * norm_gains[1]
        + mixture_raw * rms_scale(mixture_raw) * norm_gains[2]
    ).astype(jnp.bfloat16)
    upstream = cotangent.astype(jnp.float32)
    dense_grad = norm_grad(dense_raw, norm_gains[1], upstream).astype(jnp.bfloat16)
    mixture_grad = norm_grad(mixture_raw, norm_gains[2], upstream).astype(jnp.bfloat16)
    arrived_grad, dense_rows = spread(mixture_grad, pick, slot_gates, dense_grad, experts, 1)
    back_dense = jnp.einsum("gd,hd->gh", dense_rows, dense_out, preferred_element_type=jnp.float32)
    gate_dense = (back_dense * preact_dense[:, 1] * silu_grad(preact_dense[:, 0])).astype(
        jnp.bfloat16
    )
    up_dense = (back_dense * jax.nn.silu(preact_dense[:, 0])).astype(jnp.bfloat16)
    dense_input = jnp.dot(gate_dense, dense_in[0], preferred_element_type=jnp.float32) + jnp.dot(
        up_dense, dense_in[1], preferred_element_type=jnp.float32
    )
    back_expert = jnp.einsum(
        "scd,hd->sch",
        arrived_grad,
        weight_out,
        preferred_element_type=jnp.float32,
    )
    gate_expert = (back_expert * preact_expert[:, :, 1] * silu_grad(preact_expert[:, :, 0])).astype(
        jnp.bfloat16
    )
    up_expert = (back_expert * jax.nn.silu(preact_expert[:, :, 0])).astype(jnp.bfloat16)
    input_part = (
        jnp.einsum("sch,hd->scd", gate_expert, weight_in[0], preferred_element_type=jnp.float32)
        + jnp.einsum("sch,hd->scd", up_expert, weight_in[1], preferred_element_type=jnp.float32)
    ).astype(jnp.bfloat16)
    returned_grad = lax.all_to_all(input_part, "expert", split_axis=0, concat_axis=0, tiled=True)
    returned_grad = returned_grad.reshape(experts * capacity, model_width)
    mixture_input = jnp.dot(pick, returned_grad, preferred_element_type=jnp.float32)
    input_total = lax.psum_scatter(
        (dense_input + mixture_input).astype(jnp.bfloat16),
        "tensor",
        scatter_dimension=0,
        tiled=True,
    ).astype(jnp.float32)
    input_grad = norm_grad(source, norm_gains[0], input_total).astype(jnp.bfloat16)
    return (layer_output, input_grad)


def solution(mesh):
    placed = (
        P(("expert", "tensor"), None),
        P(None, "tensor", None),
        P("tensor", None),
        P("expert", None, "tensor", None),
        P("expert", "tensor", None),
        P(),
        P("expert", None),
        P("expert", None),
        P(("expert", "tensor"), None),
    )
    return jax.shard_map(
        per_device,
        mesh=mesh,
        in_specs=placed,
        out_specs=(P(("expert", "tensor"), None), P(("expert", "tensor"), None)),
        check_vma=False,
    )
```
